32 devices in a mesh: seq: 8 (over y, x, core), head: 4 (over z).
Axes of the slice: x: 2, y: 2, z: 4, core: 2. Of those that a mesh axis runs over, the one named last changes fastest.
Arguments:
- hidden: bfloat16 [4096, 4096], P(('seq', 'head')), may hold values from -6 to 6
- masked: int32 [4096], P(('seq', 'head')), may hold values 0 or 1
- mask_embed: bfloat16 [4096], replicated, may hold values from -6 to 6
- in_gain: float32 [4096], replicated, may hold values from 0.5 to 1.5
- w_gate: bfloat16 [4096, 4096], P(None, 'head'), may hold values from -0.09375 to 0.09375
- w_value: bfloat16 [4096, 4096], P(None, 'head'), may hold values from -0.09375 to 0.09375
- w_step: bfloat16 [4096, 64], P(None, 'head'), may hold values from -0.09375 to 0.09375
- w_bc: bfloat16 [4096, 256], replicated, may hold values from -0.0078125 to 0.0078125
- dt_bias_forward: float32 [64], P('head'), may hold values from -1 to 1
- dt_bias_reverse: float32 [64], P('head'), may hold values from -1 to 1
- rate_forward: float32 [64], P('head'), as said below
- rate_reverse: float32 [64], P('head'), as said below
- skip_forward: float32 [64], P('head'), may hold values from 0.5 to 1.5
- skip_reverse: float32 [64], P('head'), may hold values from 0.5 to 1.5
- out_gain: float32 [4096], P('head'), may hold values from 0.1 to 1.9
- w_out: bfloat16 [4096, 4096], P('head'), may hold values from -0.09375 to 0.09375
Outputs:
- mixed: bfloat16 [4096, 4096], P(('seq', 'head'))
The draws below stay inside these ranges and needn't reach their ends.
Inputs may be any that keep to these rules, and one draw needn't show every extreme that they name: `rate_forward`: positive decay rates of the 64 heads, each at most 0.05 a position. `rate_reverse`: positive decay rates of the 64 heads, each at most 0.05 a position.
All inputs are finite; a program needn't handle non-finite values. No bound on the sum of `masked` on one device may be relied on, other than what follows from the above.
Results may differ from the reference program's by a relative error of at most 0.014.
The reference program's roundings to bfloat16 on the way (of `source` and `normed`) count: a program that leaves them out, or rounds other values in their place, can miss the bound.
Values may be sent and summed in bfloat16 or wider, within the bound.
A program may use at most 128 MiB of HBM per device.

```python
import math
import jax
import jax.numpy as jnp
from jax import lax

D = 4096
HEADS = 64
HEAD_DIM = 64
STATE = 128
BLOCK = 256
TOKENS = 4096
INNER = 4096


def rates_from(key):
    key_order, key_level = jax.random.split(key, 2)
    order = jax.random.permutation(key_order, HEADS)
    slow_count = HEADS // 2
    slow = order < slow_count
    level = jax.random.uniform(key_level, (HEADS,), jnp.float32)
    fast_rate = jnp.exp(math.log(1.0 / 50.0) + level * (math.log(1.0 / 20.0) - math.log(1.0 / 50.0)))
    slow_rate = jnp.exp(math.log(0.1 / TOKENS) + level * math.log(10.0))
    return jnp.where(slow, slow_rate, fast_rate).astype(jnp.float32)


def draw_rate_forward(key, part):
    return rates_from(jax.random.fold_in(key, 11))


def draw_rate_reverse(key, part):
    return rates_from(jax.random.fold_in(key, 23))


def touch_ends(values, own_key, smallest, largest):
    shape = values.shape
    index_at = [jax.random.randint(jax.random.fold_in(own_key, axis), (), 0, shape[axis]) for axis in range(len(shape))]
    values = values.at[tuple(index_at)].set(smallest)
    longest = shape.index(max(shape))
    index_at[longest] = (index_at[longest] + 1) % shape[longest]
    return values.at[tuple(index_at)].set(largest)


def levels(stream_key, shape, cuts, low, high):
    loudness = 1.0
    for axis_at, parts in cuts:
        heights = jax.random.uniform(jax.random.fold_in(jax.random.fold_in(stream_key, 6), axis_at), (parts,), jnp.float32, low / len(cuts), high / len(cuts))
        loudness = loudness * jnp.repeat(jnp.exp(heights), shape[axis_at] // parts).reshape((-1,) + (1,) * (len(shape) - 1 - axis_at))
    return loudness


def centred(stream_key, dims, scale, reach, cuts=(), held_as=jnp.bfloat16):
    result = scale * jax.random.normal(stream_key, dims, jnp.float32)
    if cuts:
        result = result * levels(stream_key, dims, cuts, -0.22, 0.18)
    return jnp.clip(result, -reach, reach).astype(held_as)


def setup_inputs(seed: int = 0) -> dict:
    key_of = jax.random.split(jax.random.key(seed), 17)
    return {
        "hidden": centred(key_of[0], (TOKENS, D), 1.0, 6.0, ((0, 32),)),
        "masked": touch_ends((jax.random.randint(key_of[1], (TOKENS,), 0, 4) < 1).astype(jnp.int32), jax.random.fold_in(key_of[1], 1), 0, 1),
        "mask_embed": centred(key_of[2], (D,), 1.0, 6.0),
        "in_gain": jnp.clip(1.0 + 0.1 * jax.random.normal(key_of[3], (D,), jnp.float32), 0.5, 1.5),
        "w_gate": centred(key_of[4], (D, INNER), D ** -0.5, 0.09375, ((1, 4),)),
        "w_value": centred(key_of[5], (D, INNER), D ** -0.5, 0.09375, ((1, 4),)),
        "w_step": centred(key_of[6], (D, HEADS), D ** -0.5, 0.09375, ((1, 4),)),
        "w_bc": centred(key_of[7], (D, 2 * STATE), (D * STATE) ** -0.5, 0.0078125),
        "dt_bias_forward": jnp.clip(jax.random.uniform(key_of[8], (HEADS,), jnp.float32, -1.0, 1.0) * levels(key_of[8], (HEADS,), ((0, 4),), -0.4, 0.0), -1.0, 1.0),
        "dt_bias_reverse": jnp.clip(jax.random.uniform(key_of[9], (HEADS,), jnp.float32, -1.0, 1.0) * levels(key_of[9], (HEADS,), ((0, 4),), -0.4, 0.0), -1.0, 1.0),
        "rate_forward": draw_rate_forward(jax.random.fold_in(key_of[16], 71), 0),
        "rate_reverse": draw_rate_reverse(jax.random.fold_in(key_of[16], 71), 0),
        "skip_forward": jnp.clip(0.5 + 1.0 * jax.random.uniform(key_of[12], (HEADS,), jnp.float32) ** levels(key_of[12], (HEADS,), ((0, 4),), -0.2, 0.2), 0.5, 1.5),
        "skip_reverse": jnp.clip(0.5 + 1.0 * jax.random.uniform(key_of[13], (HEADS,), jnp.float32) ** levels(key_of[13], (HEADS,), ((0, 4),), -0.2, 0.2), 0.5, 1.5),
        "out_gain": jnp.clip(1.0 + 0.18 * jax.random.normal(key_of[14], (INNER,), jnp.float32), 0.1, 1.9),
        "w_out": centred(key_of[15], (INNER, D), INNER ** -0.5, 0.09375, ((0, 4),)),
    }


epsilon = 1e-05

def scan_direction(values, b_rows, c_rows, steps_dt, rates, skip_gain):
    total_rows = values.shape[0]
    block_count = total_rows // BLOCK
    heads_all = values.shape[1]
    tri_mask = jnp.arange(BLOCK)[:, None] >= jnp.arange(BLOCK)[None, :]
    log_decay = -rates[None, :] * steps_dt

    def one_block(state, pieces):
        val_blk, b_blk, c_blk, log_blk, step_blk = pieces
        cumul = jnp.cumsum(log_blk, axis=0)
        cumul_heads = cumul.T
        differ = cumul_heads[:, :, None] - cumul_heads[:, None, :]
        weights = jnp.exp(jnp.where(tri_mask[None], differ, -jnp.inf)) * step_blk.T[:, None, :]
        scores = jnp.dot(c_blk, b_blk.T, preferred_element_type=jnp.float32)
        mixing = lax.optimization_barrier((scores[None] * weights).astype(jnp.bfloat16))
        inside = jnp.einsum('hts,shp->thp', mixing.astype(jnp.float32), val_blk.astype(jnp.float32))
        entering = lax.optimization_barrier(state.astype(jnp.bfloat16))
        carried = jnp.einsum('tn,hpn->thp', c_blk.astype(jnp.float32), entering.astype(jnp.float32))
        carried = carried * jnp.exp(cumul)[:, :, None]
        to_end = jnp.exp(cumul[-1][None, :] - cumul) * step_blk
        scaled = lax.optimization_barrier((val_blk.astype(jnp.float32) * to_end[:, :, None]).astype(jnp.bfloat16))
        block_state = jnp.einsum('shp,sn->hpn', scaled.astype(jnp.float32), b_blk.astype(jnp.float32))
        new_state = jnp.exp(cumul[-1])[:, None, None] * state + block_state
        output = inside + carried + skip_gain[None, :, None] * val_blk.astype(jnp.float32)
        return (new_state, output)
    pieces = (values.reshape(block_count, BLOCK, heads_all, HEAD_DIM), b_rows.reshape(block_count, BLOCK, STATE), c_rows.reshape(block_count, BLOCK, STATE), log_decay.reshape(block_count, BLOCK, heads_all), steps_dt.reshape(block_count, BLOCK, heads_all))
    start_state = jnp.zeros((heads_all, HEAD_DIM, STATE), jnp.float32)
    _, outputs = lax.scan(one_block, start_state, pieces)
    return outputs.reshape(total_rows, heads_all * HEAD_DIM)

def gated_norm(output, gate_act, out_gain):
    gated = output * gate_act
    scale = lax.rsqrt(lax.optimization_barrier(jnp.mean(gated * gated, axis=1, keepdims=True)) + epsilon)
    return (gated * scale * out_gain[None, :]).astype(jnp.bfloat16)

def reference(hidden, masked, mask_embed, in_gain, w_gate, w_value, w_step, w_bc, dt_bias_forward, dt_bias_reverse, rate_forward, rate_reverse, skip_forward, skip_reverse, out_gain, w_out):
    source = jnp.where(masked[:, None] == 1, mask_embed[None, :], hidden)
    source_f = source.astype(jnp.float32)
    normed = (source_f * lax.rsqrt(lax.optimization_barrier(jnp.mean(source_f * source_f, axis=1, keepdims=True)) + epsilon) * in_gain[None, :]).astype(jnp.bfloat16)
    gate_proj = jnp.dot(normed, w_gate, preferred_element_type=jnp.float32)
    value_proj = jnp.dot(normed, w_value, preferred_element_type=jnp.float32)
    step_proj = jnp.dot(normed, w_step, preferred_element_type=jnp.float32)
    bc_proj = jnp.dot(normed, w_bc, preferred_element_type=jnp.float32)
    values = jax.nn.silu(value_proj).astype(jnp.bfloat16).reshape(normed.shape[0], HEADS, HEAD_DIM)
    b_rows = bc_proj[:, :STATE].astype(jnp.bfloat16)
    c_rows = bc_proj[:, STATE:].astype(jnp.bfloat16)
    dt_forward = jax.nn.softplus(step_proj + dt_bias_forward[None, :])
    dt_reverse = jax.nn.softplus(step_proj + dt_bias_reverse[None, :])
    forward_out = scan_direction(values, b_rows, c_rows, dt_forward, rate_forward, skip_forward)
    reverse_out = scan_direction(values[::-1], b_rows[::-1], c_rows[::-1], dt_reverse[::-1], rate_reverse, skip_reverse)[::-1]
    gate_act = jax.nn.silu(gate_proj)
    normed_forward = gated_norm(forward_out, gate_act, out_gain)
    normed_reverse = gated_norm(reverse_out, gate_act, out_gain)
    total = jnp.dot(normed_forward, w_out, preferred_element_type=jnp.float32) + jnp.dot(normed_reverse, w_out, preferred_element_type=jnp.float32)
    return total.astype(jnp.bfloat16)
```

```python
import jax
import jax.numpy as jnp
from jax import lax
from jax.sharding import PartitionSpec as P

HEADS = 64
HEAD_DIM = 64
STATE = 128
BLOCK = 256

epsilon = 1e-05
bf16 = jnp.bfloat16
f32 = jnp.float32


def dot(a, b):
    return jnp.dot(a, b, preferred_element_type=f32)


def direction_terms(values, b_blk, scores, steps_dt, rates, reverse):
    block_count, size, head_count, _ = values.shape
    step_blk = steps_dt.reshape(block_count, size, head_count)
    logd = -rates * step_blk
    at = jnp.arange(size)
    keep = at[:, None] <= at[None, :] if reverse else at[:, None] >= at[None, :]
    cum = jnp.einsum(
        "ts,bsh->bth", keep.astype(f32), logd, precision=lax.Precision.HIGHEST
    )
    total = cum[:, 0] if reverse else cum[:, -1]
    cum_h = jnp.swapaxes(cum, 1, 2)
    differ = cum_h[:, :, :, None] - cum_h[:, :, None, :]
    weights = (
        jnp.exp(jnp.where(keep, differ, -jnp.inf)) * jnp.swapaxes(step_blk, 1, 2)[:, :, None, :]
    )
    mixing = (scores[:, None] * weights).astype(bf16)
    inside = jnp.einsum("bhts,bshp->bthp", mixing, values, preferred_element_type=f32)
    to_end = jnp.exp(total[:, None] - cum) * step_blk
    scaled = (values.astype(f32) * to_end[..., None]).astype(bf16)
    states = jnp.einsum("bshp,bsn->bhpn", scaled, b_blk, preferred_element_type=f32)
    order = range(block_count - 1, -1, -1) if reverse else range(block_count)
    starts, prefix = [None] * block_count, [None] * block_count
    running, product = jnp.zeros_like(states[0]), jnp.zeros_like(total[0])
    for i in order:
        starts[i], prefix[i] = running, product
        running = jnp.exp(total[i])[:, None, None] * running + states[i]
        product = product + total[i]
    return inside, cum, jnp.stack(starts), jnp.stack(prefix), running, product


def entering(gathered, logs, place, reverse):
    count = gathered.shape[0]
    at = jnp.arange(count)
    if reverse:
        between = (at[None, :] < at[:, None]) & (at[None, :] > place)
        used = at > place
    else:
        between = (at[None, :] > at[:, None]) & (at[None, :] < place)
        used = at < place
    decay = jnp.sum(jnp.where(between[:, :, None], logs[None], 0.0), axis=1)
    factor = jnp.where(used[:, None], jnp.exp(decay), 0.0)
    return jnp.sum(factor[:, :, None, None] * gathered.astype(f32), axis=0)


def on_device(
    hidden, masked, mask_embed, in_gain, w_gate, w_value, w_step, w_bc,
    dt_bias_forward, dt_bias_reverse, rate_forward, rate_reverse,
    skip_forward, skip_reverse, out_gain, w_out,
):
    source = jnp.where(masked[:, None] == 1, mask_embed[None, :], hidden).astype(f32)
    normed = (
        source
        * lax.rsqrt(jnp.mean(source * source, axis=1, keepdims=True) + epsilon)
        * in_gain[None, :]
    ).astype(bf16)
    rows = lax.all_gather(normed, "head", axis=0, tiled=True)
    gate_act = jax.nn.silu(dot(rows, w_gate))
    step_proj = dot(rows, w_step)
    row_count, head_count = step_proj.shape
    block_count = row_count // BLOCK
    values = jax.nn.silu(dot(rows, w_value)).astype(bf16)
    values = values.reshape(block_count, BLOCK, head_count, HEAD_DIM)
    bc = dot(rows, w_bc).astype(bf16).reshape(block_count, BLOCK, 2 * STATE)
    b_blk, c_blk = bc[..., :STATE], bc[..., STATE:]
    scores = jnp.einsum("btn,bsn->bts", c_blk, b_blk, preferred_element_type=f32)
    dt_f = jax.nn.softplus(step_proj + dt_bias_forward)
    dt_r = jax.nn.softplus(step_proj + dt_bias_reverse)
    terms_f = direction_terms(values, b_blk, scores, dt_f, rate_forward, False)
    terms_r = direction_terms(values, b_blk, scores, dt_r, rate_reverse, True)
    ends = jnp.stack([terms_f[4], terms_r[4]]).astype(bf16)
    logs = lax.all_gather(jnp.stack([terms_f[5], terms_r[5]]), "seq")
    ends = lax.all_gather(ends, "seq")
    place = lax.axis_index("seq")
    gated = []
    for i, (terms, skip) in enumerate(((terms_f, skip_forward), (terms_r, skip_reverse))):
        inside, cum, starts, prefix = terms[:4]
        enter = entering(ends[:, i], logs[:, i], place, i == 1)
        states = (starts + jnp.exp(prefix)[:, :, None, None] * enter[None]).astype(bf16)
        carried = jnp.einsum("btn,bhpn->bthp", c_blk, states, preferred_element_type=f32)
        out = inside + carried * jnp.exp(cum)[..., None] + skip[:, None] * values.astype(f32)
        gated.append(out.reshape(row_count, -1) * gate_act)
    totals = lax.psum(jnp.stack([jnp.sum(g * g, axis=1) for g in gated]), "head")
    inner = HEADS * HEAD_DIM
    scale = lax.rsqrt(totals / inner + epsilon)
    both = gated[0] * scale[0][:, None] + gated[1] * scale[1][:, None]
    both = (both * out_gain[None, :]).astype(bf16)
    part = dot(both, w_out).astype(bf16)
    return lax.psum_scatter(part, "head", scatter_dimension=0, tiled=True)


def solution(mesh):
    head = P("head")
    in_specs = (
        P(("seq", "head"), None), P(("seq", "head")), P(), P(),
        P(None, "head"), P(None, "head"), P(None, "head"), P(),
        head, head, head, head, head, head, head, P("head", None),
    )
    return jax.shard_map(
        on_device, mesh=mesh, in_specs=in_specs,
        out_specs=P(("seq", "head"), None), check_vma=False,
    )
```

```python
import functools

import jax
import jax.numpy as jnp
from jax import lax
from jax.experimental import pallas as pl
from jax.experimental.pallas import tpu as pltpu
from jax.sharding import PartitionSpec as P

HEADS = 64
HEAD_DIM = 64
STATE = 128
BLOCK = 256

epsilon = 1e-05
bf16 = jnp.bfloat16
f32 = jnp.float32
MESH = pl.DeviceIdType.MESH


def dot(a, b):
    return jnp.dot(a, b, preferred_element_type=f32)


def line_barrier(axis, n):
    me = lax.axis_index(axis)
    barrier = pltpu.get_barrier_semaphore()
    for other in range(1, n):
        pl.semaphore_signal(
            barrier, inc=1, device_id={axis: lax.rem(me + other, n)}, device_id_type=MESH
        )
    pl.semaphore_wait(barrier, n - 1)


def project_kernel(
    n, subs, hidden, masked, embed, in_gain, gate_hbm, value_hbm, step_hbm, bc_hbm,
    gate_out, value_out, step_out, bc_out,
    rows, w_gate, w_value, w_step, w_bc, load_sem, right_sem, left_sem, recv_sem,
):
    me = lax.axis_index("head")
    loads = [
        pltpu.make_async_copy(src, dst, load_sem.at[i])
        for i, (src, dst) in enumerate(
            ((bc_hbm, w_bc), (step_hbm, w_step), (value_hbm, w_value), (gate_hbm, w_gate))
        )
    ]
    for load in loads:
        load.start()
    count = hidden.shape[0]
    part = count // subs

    def copy(chunk, sub, send_sem, target):
        piece = rows.at[chunk, pl.ds(sub * part, part)]
        return pltpu.make_async_remote_copy(
            src_ref=piece, dst_ref=piece, send_sem=send_sem.at[chunk, sub],
            recv_sem=recv_sem.at[chunk, sub],
            device_id={"head": target}, device_id_type=MESH,
        )

    line_barrier("head", n)
    for sub in range(subs):
        own = pl.ds(sub * part, part)
        source = jnp.where(masked[own, :] == 1, embed[...], hidden[own, :]).astype(f32)
        mean = jnp.mean(source * source, axis=1, keepdims=True)
        rows[me, own, :] = (source * lax.rsqrt(mean + epsilon) * in_gain[...]).astype(bf16)

        @pl.when(me < n - 1)
        def _():
            copy(me, sub, right_sem, me + 1).start()

        @pl.when(me > 0)
        def _():
            copy(me, sub, left_sem, me - 1).start()

    for load in loads:
        load.wait()

    def compute(chunk):
        x = rows[chunk]
        at = pl.ds(pl.multiple_of(chunk * count, count), count)
        bc_out[at, :] = dot(x, w_bc[...]).astype(bf16)
        step_out[at, :] = dot(x, w_step[...])
        width = w_gate.shape[1]
        tile = 256 if width % 256 == 0 else width

        @pl.loop(0, width // tile)
        def _(i):
            cols = pl.ds(pl.multiple_of(i * tile, tile), tile)
            v = dot(x, w_value[:, cols])
            value_out[at, cols] = (v * jax.nn.sigmoid(v)).astype(bf16)
            g = dot(x, w_gate[:, cols])
            gate_out[at, cols] = (g * jax.nn.sigmoid(g)).astype(bf16)

    compute(me)

    @pl.loop(1, n)
    def _(d):
        @pl.when(me - d >= 0)
        def _():
            for sub in range(subs):
                copy(me - d, sub, right_sem, me).wait_recv()

                @pl.when(me < n - 1)
                def _():
                    copy(me - d, sub, right_sem, me + 1).start()

        @pl.when(me + d < n)
        def _():
            for sub in range(subs):
                copy(me + d, sub, left_sem, me).wait_recv()

                @pl.when(me > 0)
                def _():
                    copy(me + d, sub, left_sem, me - 1).start()

        @pl.when(me - d >= 0)
        def _():
            compute(me - d)

        @pl.when(me + d < n)
        def _():
            compute(me + d)

    @pl.loop(0, n)
    def _(c):
        @pl.when((c <= me) & (me < n - 1))
        def _():
            for sub in range(subs):
                copy(c, sub, right_sem, me + 1).wait_send()

        @pl.when((c >= me) & (me > 0))
        def _():
            for sub in range(subs):
                copy(c, sub, left_sem, me - 1).wait_send()


def project(n, hidden, masked, mask_embed, in_gain, w_gate, w_value, w_step, w_bc):
    count, width = hidden.shape
    units, heads, both = w_gate.shape[1], w_step.shape[1], w_bc.shape[1]
    subs = 2
    total = n * count
    vmem, any_ = pl.BlockSpec(memory_space=pltpu.VMEM), pl.BlockSpec(memory_space=pl.ANY)
    sems = pltpu.SemaphoreType.DMA((n, subs))
    return pl.pallas_call(
        functools.partial(project_kernel, n, subs),
        out_shape=(
            jax.ShapeDtypeStruct((total, units), bf16),
            jax.ShapeDtypeStruct((total, units), bf16),
            jax.ShapeDtypeStruct((total, heads), f32),
            jax.ShapeDtypeStruct((total, both), bf16),
        ),
        in_specs=[vmem] * 4 + [any_] * 4,
        out_specs=(vmem,) * 4,
        scratch_shapes=[
            pltpu.VMEM((n, count, width), bf16),
            pltpu.VMEM(w_gate.shape, bf16), pltpu.VMEM(w_value.shape, bf16),
            pltpu.VMEM(w_step.shape, bf16), pltpu.VMEM(w_bc.shape, bf16),
            pltpu.SemaphoreType.DMA((4,)), sems, sems, sems,
        ],
        compiler_params=pltpu.CompilerParams(
            collective_id=0, has_side_effects=True, vmem_limit_bytes=56 * 2**20
        ),
    )(hidden, masked[:, None], mask_embed[None], in_gain[None], w_gate, w_value, w_step, w_bc)


def output_kernel(
    n, subs, inner, gated_f, gated_r, gain, w_hbm, out,
    w_out, both, sums, held, sent, load_sem, sum_send, sum_recv, send_sem, recv_sem,
):
    me = lax.axis_index("head")
    load = pltpu.make_async_copy(w_hbm, w_out, load_sem)
    load.start()
    count = out.shape[0]
    part = out.shape[1] // subs
    ones = jnp.ones((8, gated_f.shape[1]), f32)

    def row_sums(ref):
        g = ref[...]
        return lax.dot_general(
            ones, g * g, (((1,), (1,)), ((), ())),
            precision=lax.Precision.HIGHEST, preferred_element_type=f32,
        )

    sums[me, 0:8, :] = row_sums(gated_f)
    sums[me, 8:16, :] = row_sums(gated_r)
    line_barrier("head", n)

    def share(owner, target, slot):
        return pltpu.make_async_remote_copy(
            src_ref=sums.at[owner], dst_ref=sums.at[owner], send_sem=sum_send.at[slot],
            recv_sem=sum_recv.at[owner], device_id={"head": target}, device_id_type=MESH,
        )

    for other in range(1, n):
        share(me, lax.rem(me + other, n), other).start()
    for other in range(1, n):
        owner = lax.rem(me + other, n)
        share(owner, owner, other).wait_recv()
    total = jnp.sum(sums[...], axis=0)
    scale = lax.rsqrt(total / inner + epsilon).T
    mixed = gated_f[...] * scale[:, 0:1] + gated_r[...] * scale[:, 8:9]
    both[...] = (mixed * gain[...]).astype(bf16)
    load.wait()

    def partial(dest, sub):
        at = pl.ds(pl.multiple_of(dest * count, count), count)
        return dot(both[at, :], w_out[:, pl.ds(pl.multiple_of(sub * part, part), part)])

    def send(dest, sub, way, target):
        return pltpu.make_async_remote_copy(
            src_ref=sent.at[dest, sub], dst_ref=held.at[way, dest, sub],
            send_sem=send_sem.at[dest, sub], recv_sem=recv_sem.at[way, dest, sub],
            device_id={"head": target}, device_id_type=MESH,
        )

    def pass_on(dest, sub, way, first, target):
        sent[dest, sub] = partial(dest, sub).astype(bf16)

        @pl.when(jnp.logical_not(first))
        def _():
            send(dest, sub, way, me).wait_recv()
            sent[dest, sub] = (
                sent[dest, sub].astype(f32) + held[way, dest, sub].astype(f32)
            ).astype(bf16)

        send(dest, sub, way, target).start()

    @pl.loop(0, (n - 1) * subs)
    def _(i):
        t, sub = i // subs, lax.rem(i, subs)

        @pl.when((t >= me) & (me < n - 1))
        def _():
            pass_on(n - 1 - t + me, sub, 0, me == 0, me + 1)

        @pl.when((t >= n - 1 - me) & (me > 0))
        def _():
            pass_on(t - (n - 1 - me), sub, 1, me == n - 1, me - 1)

    @pl.loop(0, subs)
    def _(sub):
        cols = pl.ds(pl.multiple_of(sub * part, part), part)
        out[:, cols] = partial(me, sub).astype(bf16)

        @pl.when(me > 0)
        def _():
            send(me, sub, 0, me).wait_recv()
            out[:, cols] = (out[:, cols].astype(f32) + held[0, me, sub].astype(f32)).astype(bf16)

        @pl.when(me < n - 1)
        def _():
            send(me, sub, 1, me).wait_recv()
            out[:, cols] = (out[:, cols].astype(f32) + held[1, me, sub].astype(f32)).astype(bf16)

    @pl.loop(0, n * subs)
    def _(i):
        dest, sub = i // subs, lax.rem(i, subs)

        @pl.when(dest != me)
        def _():
            send(dest, sub, 0, me).wait_send()

    for other in range(1, n):
        share(me, me, other).wait_send()


def project_out(n, inner, gated_f, gated_r, out_gain, w_out):
    rows, units = gated_f.shape
    width = w_out.shape[1]
    count = rows // n
    subs = 4
    vmem, any_ = pl.BlockSpec(memory_space=pltpu.VMEM), pl.BlockSpec(memory_space=pl.ANY)
    return pl.pallas_call(
        functools.partial(output_kernel, n, subs, inner),
        out_shape=jax.ShapeDtypeStruct((count, width), bf16),
        in_specs=[vmem] * 3 + [any_],
        out_specs=vmem,
        scratch_shapes=[
            pltpu.VMEM(w_out.shape, bf16),
            pltpu.VMEM((rows, units), bf16),
            pltpu.VMEM((n, 16, rows), f32),
            pltpu.VMEM((2, n, subs, count, width // subs), bf16),
            pltpu.VMEM((n, subs, count, width // subs), bf16),
            pltpu.SemaphoreType.DMA, pltpu.SemaphoreType.DMA((n,)),
            pltpu.SemaphoreType.DMA((n,)), pltpu.SemaphoreType.DMA((n, subs)),
            pltpu.SemaphoreType.DMA((2, n, subs)),
        ],
        compiler_params=pltpu.CompilerParams(
            collective_id=1, has_side_effects=True, vmem_limit_bytes=56 * 2**20
        ),
    )(gated_f, gated_r, out_gain[None], w_out)


def direction_terms(values, b_blk, scores, steps_dt, rates, reverse):
    block_count, size, head_count, _ = values.shape
    step_blk = steps_dt.reshape(block_count, size, head_count)
    logd = -rates * step_blk
    at = jnp.arange(size)
    keep = at[:, None] <= at[None, :] if reverse else at[:, None] >= at[None, :]
    cum = jnp.einsum(
        "ts,bsh->bth", keep.astype(f32), logd, precision=lax.Precision.HIGHEST
    )
    total = cum[:, 0] if reverse else cum[:, -1]
    cum_h = jnp.swapaxes(cum, 1, 2)
    differ = cum_h[:, :, :, None] - cum_h[:, :, None, :]
    weights = (
        jnp.exp(jnp.where(keep, differ, -jnp.inf)) * jnp.swapaxes(step_blk, 1, 2)[:, :, None, :]
    )
    mixing = (scores[:, None] * weights).astype(bf16)
    inside = jnp.einsum("bhts,bshp->bthp", mixing, values, preferred_element_type=f32)
    to_end = jnp.exp(total[:, None] - cum) * step_blk
    scaled = (values.astype(f32) * to_end[..., None]).astype(bf16)
    states = jnp.einsum("bshp,bsn->bhpn", scaled, b_blk, preferred_element_type=f32)
    order = range(block_count - 1, -1, -1) if reverse else range(block_count)
    starts, prefix = [None] * block_count, [None] * block_count
    running, product = jnp.zeros_like(states[0]), jnp.zeros_like(total[0])
    for i in order:
        starts[i], prefix[i] = running, product
        running = jnp.exp(total[i])[:, None, None] * running + states[i]
        product = product + total[i]
    return inside, cum, jnp.stack(starts), jnp.stack(prefix), running, product


def entering(gathered, logs, place, reverse):
    count = gathered.shape[0]
    at = jnp.arange(count)
    if reverse:
        between = (at[None, :] < at[:, None]) & (at[None, :] > place)
        used = at > place
    else:
        between = (at[None, :] > at[:, None]) & (at[None, :] < place)
        used = at < place
    decay = jnp.sum(jnp.where(between[:, :, None], logs[None], 0.0), axis=1)
    factor = jnp.where(used[:, None], jnp.exp(decay), 0.0)
    return jnp.sum(factor[:, :, None, None] * gathered.astype(f32), axis=0)


def on_device(
    hidden, masked, mask_embed, in_gain, w_gate, w_value, w_step, w_bc,
    dt_bias_forward, dt_bias_reverse, rate_forward, rate_reverse,
    skip_forward, skip_reverse, out_gain, w_out,
):
    n = lax.axis_size("head")
    gate_act, values, step_proj, bc = project(
        n, hidden, masked, mask_embed, in_gain, w_gate, w_value, w_step, w_bc
    )
    row_count, head_count = step_proj.shape
    block_count = row_count // BLOCK
    values = values.reshape(block_count, BLOCK, head_count, HEAD_DIM)
    bc = bc.reshape(block_count, BLOCK, 2 * STATE)
    b_blk, c_blk = bc[..., :STATE], bc[..., STATE:]
    scores = jnp.einsum("btn,bsn->bts", c_blk, b_blk, preferred_element_type=f32)
    dt_f = jax.nn.softplus(step_proj + dt_bias_forward)
    dt_r = jax.nn.softplus(step_proj + dt_bias_reverse)
    terms_f = direction_terms(values, b_blk, scores, dt_f, rate_forward, False)
    terms_r = direction_terms(values, b_blk, scores, dt_r, rate_reverse, True)
    ends = jnp.stack([terms_f[4], terms_r[4]]).astype(bf16)
    logs = lax.all_gather(jnp.stack([terms_f[5], terms_r[5]]), "seq")
    ends = lax.all_gather(ends, "seq")
    place = lax.axis_index("seq")
    gated = []
    for i, (terms, skip) in enumerate(((terms_f, skip_forward), (terms_r, skip_reverse))):
        inside, cum, starts, prefix = terms[:4]
        enter = entering(ends[:, i], logs[:, i], place, i == 1)
        states = (starts + jnp.exp(prefix)[:, :, None, None] * enter[None]).astype(bf16)
        carried = jnp.einsum("btn,bhpn->bthp", c_blk, states, preferred_element_type=f32)
        out = inside + carried * jnp.exp(cum)[..., None] + skip[:, None] * values.astype(f32)
        gated.append(out.reshape(row_count, -1) * gate_act)
    return project_out(n, HEADS * HEAD_DIM, gated[0], gated[1], out_gain, w_out)


def solution(mesh):
    head = P("head")
    in_specs = (
        P(("seq", "head"), None), P(("seq", "head")), P(), P(),
        P(None, "head"), P(None, "head"), P(None, "head"), P(),
        head, head, head, head, head, head, head, P("head", None),
    )
    return jax.shard_map(
        on_device, mesh=mesh, in_specs=in_specs,
        out_specs=P(("seq", "head"), None), check_vma=False,
    )
```

```python
import functools

import jax
import jax.numpy as jnp
from jax import lax
from jax.experimental import pallas as pl
from jax.experimental.pallas import tpu as pltpu
from jax.sharding import PartitionSpec as P

HEADS = 64
HEAD_DIM = 64
STATE = 128
BLOCK = 256
LANES = 128

epsilon = 1e-05
bf16 = jnp.bfloat16
f32 = jnp.float32
MESH = pl.DeviceIdType.MESH


def dot(a, b):
    return jnp.dot(a, b, preferred_element_type=f32)


def line_barrier(axis, n):
    me = lax.axis_index(axis)
    barrier = pltpu.get_barrier_semaphore()
    for other in range(1, n):
        pl.semaphore_signal(
            barrier, inc=1, device_id={axis: lax.rem(me + other, n)}, device_id_type=MESH
        )
    pl.semaphore_wait(barrier, n - 1)


def project_kernel(
    n, subs, hidden, masked, embed, in_gain, gate_hbm, value_hbm, step_hbm, bc_hbm,
    gate_out, value_out, step_out, bc_out,
    rows, w_gate, w_value, w_step, w_bc, load_sem, right_sem, left_sem, recv_sem,
):
    me = lax.axis_index("head")
    loads = [
        pltpu.make_async_copy(src, dst, load_sem.at[i])
        for i, (src, dst) in enumerate(
            ((bc_hbm, w_bc), (step_hbm, w_step), (value_hbm, w_value), (gate_hbm, w_gate))
        )
    ]
    for load in loads:
        load.start()
    count = hidden.shape[0]
    part = count // subs

    def copy(chunk, sub, send_sem, target):
        piece = rows.at[chunk, pl.ds(sub * part, part)]
        return pltpu.make_async_remote_copy(
            src_ref=piece, dst_ref=piece, send_sem=send_sem.at[chunk, sub],
            recv_sem=recv_sem.at[chunk, sub],
            device_id={"head": target}, device_id_type=MESH,
        )

    line_barrier("head", n)
    for sub in range(subs):
        own = pl.ds(sub * part, part)
        source = jnp.where(masked[own, :] == 1, embed[...], hidden[own, :]).astype(f32)
        mean = jnp.mean(source * source, axis=1, keepdims=True)
        rows[me, own, :] = (source * lax.rsqrt(mean + epsilon) * in_gain[...]).astype(bf16)

        @pl.when(me < n - 1)
        def _():
            copy(me, sub, right_sem, me + 1).start()

        @pl.when(me > 0)
        def _():
            copy(me, sub, left_sem, me - 1).start()

    for load in loads:
        load.wait()

    def compute(chunk):
        x = rows[chunk]
        at = pl.ds(pl.multiple_of(chunk * count, count), count)
        bc_out[at, :] = dot(x, w_bc[...]).astype(bf16)
        step_out[at, :] = dot(x, w_step[...])
        width = w_gate.shape[1]
        tile = 256 if width % 256 == 0 else width

        @pl.loop(0, width // tile)
        def _(i):
            cols = pl.ds(pl.multiple_of(i * tile, tile), tile)
            v = dot(x, w_value[:, cols])
            value_out[at, cols] = (v * jax.nn.sigmoid(v)).astype(bf16)
            g = dot(x, w_gate[:, cols])
            gate_out[at, cols] = (g * jax.nn.sigmoid(g)).astype(bf16)

    compute(me)

    @pl.loop(1, n)
    def _(d):
        @pl.when(me - d >= 0)
        def _():
            for sub in range(subs):
                copy(me - d, sub, right_sem, me).wait_recv()

                @pl.when(me < n - 1)
                def _():
                    copy(me - d, sub, right_sem, me + 1).start()

        @pl.when(me + d < n)
        def _():
            for sub in range(subs):
                copy(me + d, sub, left_sem, me).wait_recv()

                @pl.when(me > 0)
                def _():
                    copy(me + d, sub, left_sem, me - 1).start()

        @pl.when(me - d >= 0)
        def _():
            compute(me - d)

        @pl.when(me + d < n)
        def _():
            compute(me + d)

    @pl.loop(0, n)
    def _(c):
        @pl.when((c <= me) & (me < n - 1))
        def _():
            for sub in range(subs):
                copy(c, sub, right_sem, me + 1).wait_send()

        @pl.when((c >= me) & (me > 0))
        def _():
            for sub in range(subs):
                copy(c, sub, left_sem, me - 1).wait_send()


def project(n, hidden, masked, mask_embed, in_gain, w_gate, w_value, w_step, w_bc):
    count, width = hidden.shape
    units, heads, both = w_gate.shape[1], w_step.shape[1], w_bc.shape[1]
    subs = 2
    total = n * count
    vmem, any_ = pl.BlockSpec(memory_space=pltpu.VMEM), pl.BlockSpec(memory_space=pl.ANY)
    sems = pltpu.SemaphoreType.DMA((n, subs))
    return pl.pallas_call(
        functools.partial(project_kernel, n, subs),
        out_shape=(
            jax.ShapeDtypeStruct((total, units), bf16),
            jax.ShapeDtypeStruct((total, units), bf16),
            jax.ShapeDtypeStruct((total, heads), f32),
            jax.ShapeDtypeStruct((total, both), bf16),
        ),
        in_specs=[vmem] * 4 + [any_] * 4,
        out_specs=(vmem,) * 4,
        scratch_shapes=[
            pltpu.VMEM((n, count, width), bf16),
            pltpu.VMEM(w_gate.shape, bf16), pltpu.VMEM(w_value.shape, bf16),
            pltpu.VMEM(w_step.shape, bf16), pltpu.VMEM(w_bc.shape, bf16),
            pltpu.SemaphoreType.DMA((4,)), sems, sems, sems,
        ],
        compiler_params=pltpu.CompilerParams(
            collective_id=0, has_side_effects=True, vmem_limit_bytes=56 * 2**20
        ),
    )(hidden, masked[:, None], mask_embed[None], in_gain[None], w_gate, w_value, w_step, w_bc)


def output_kernel(
    n, subs, inner, gated_f, gated_r, gain, w_hbm, out,
    w_out, both, sums, held, sent, load_sem, sum_send, sum_recv, send_sem, recv_sem,
):
    me = lax.axis_index("head")
    load = pltpu.make_async_copy(w_hbm, w_out, load_sem)
    load.start()
    count = out.shape[0]
    part = out.shape[1] // subs
    ones = jnp.ones((8, gated_f.shape[1]), f32)

    def row_sums(ref):
        g = ref[...]
        return lax.dot_general(
            ones, g * g, (((1,), (1,)), ((), ())),
            precision=lax.Precision.HIGHEST, preferred_element_type=f32,
        )

    sums[me, 0:8, :] = row_sums(gated_f)
    sums[me, 8:16, :] = row_sums(gated_r)
    line_barrier("head", n)

    def share(owner, target, slot):
        return pltpu.make_async_remote_copy(
            src_ref=sums.at[owner], dst_ref=sums.at[owner], send_sem=sum_send.at[slot],
            recv_sem=sum_recv.at[owner], device_id={"head": target}, device_id_type=MESH,
        )

    for other in range(1, n):
        share(me, lax.rem(me + other, n), other).start()
    for other in range(1, n):
        owner = lax.rem(me + other, n)
        share(owner, owner, other).wait_recv()
    total = jnp.sum(sums[...], axis=0)
    scale = lax.rsqrt(total / inner + epsilon).T
    mixed = gated_f[...] * scale[:, 0:1] + gated_r[...] * scale[:, 8:9]
    both[...] = (mixed * gain[...]).astype(bf16)
    load.wait()

    def partial(dest, sub):
        at = pl.ds(pl.multiple_of(dest * count, count), count)
        return dot(both[at, :], w_out[:, pl.ds(pl.multiple_of(sub * part, part), part)])

    def send(dest, sub, way, target):
        return pltpu.make_async_remote_copy(
            src_ref=sent.at[dest, sub], dst_ref=held.at[way, dest, sub],
            send_sem=send_sem.at[dest, sub], recv_sem=recv_sem.at[way, dest, sub],
            device_id={"head": target}, device_id_type=MESH,
        )

    def pass_on(dest, sub, way, first, target):
        sent[dest, sub] = partial(dest, sub).astype(bf16)

        @pl.when(jnp.logical_not(first))
        def _():
            send(dest, sub, way, me).wait_recv()
            sent[dest, sub] = (
                sent[dest, sub].astype(f32) + held[way, dest, sub].astype(f32)
            ).astype(bf16)

        send(dest, sub, way, target).start()

    @pl.loop(0, (n - 1) * subs)
    def _(i):
        t, sub = i // subs, lax.rem(i, subs)

        @pl.when((t >= me) & (me < n - 1))
        def _():
            pass_on(n - 1 - t + me, sub, 0, me == 0, me + 1)

        @pl.when((t >= n - 1 - me) & (me > 0))
        def _():
            pass_on(t - (n - 1 - me), sub, 1, me == n - 1, me - 1)

    @pl.loop(0, subs)
    def _(sub):
        cols = pl.ds(pl.multiple_of(sub * part, part), part)
        out[:, cols] = partial(me, sub).astype(bf16)

        @pl.when(me > 0)
        def _():
            send(me, sub, 0, me).wait_recv()
            out[:, cols] = (out[:, cols].astype(f32) + held[0, me, sub].astype(f32)).astype(bf16)

        @pl.when(me < n - 1)
        def _():
            send(me, sub, 1, me).wait_recv()
            out[:, cols] = (out[:, cols].astype(f32) + held[1, me, sub].astype(f32)).astype(bf16)

    @pl.loop(0, n * subs)
    def _(i):
        dest, sub = i // subs, lax.rem(i, subs)

        @pl.when(dest != me)
        def _():
            send(dest, sub, 0, me).wait_send()

    for other in range(1, n):
        share(me, me, other).wait_send()


def project_out(n, inner, gated_f, gated_r, out_gain, w_out):
    rows, units = gated_f.shape
    width = w_out.shape[1]
    count = rows // n
    subs = 4
    vmem, any_ = pl.BlockSpec(memory_space=pltpu.VMEM), pl.BlockSpec(memory_space=pl.ANY)
    return pl.pallas_call(
        functools.partial(output_kernel, n, subs, inner),
        out_shape=jax.ShapeDtypeStruct((count, width), bf16),
        in_specs=[vmem] * 3 + [any_],
        out_specs=vmem,
        scratch_shapes=[
            pltpu.VMEM(w_out.shape, bf16),
            pltpu.VMEM((rows, units), bf16),
            pltpu.VMEM((n, 16, rows), f32),
            pltpu.VMEM((2, n, subs, count, width // subs), bf16),
            pltpu.VMEM((n, subs, count, width // subs), bf16),
            pltpu.SemaphoreType.DMA, pltpu.SemaphoreType.DMA((n,)),
            pltpu.SemaphoreType.DMA((n,)), pltpu.SemaphoreType.DMA((n, subs)),
            pltpu.SemaphoreType.DMA((2, n, subs)),
        ],
        compiler_params=pltpu.CompilerParams(
            collective_id=1, has_side_effects=True, vmem_limit_bytes=56 * 2**20
        ),
    )(gated_f, gated_r, out_gain[None], w_out)


def expand(x, spread):
    high = x.astype(bf16)
    return dot(high, spread) + dot((x - high.astype(f32)).astype(bf16), spread)


def scan_kernel(
    count, heads, values, gate, step, bc, params, gated_f, gated_r,
    cums, cums_t, dts_t, ends_log, states, mine, my_logs, held, logs, enter,
    send_sem, recv_sem, log_send, log_recv,
):
    place = lax.axis_index("seq")
    rows, units = values.shape
    blocks = rows // BLOCK
    lane_of = lax.broadcasted_iota(jnp.int32, (LANES, units), 1)
    head_of = lax.broadcasted_iota(jnp.int32, (LANES, units), 0) * HEAD_DIM
    spread = ((lane_of >= head_of) & (lane_of < head_of + HEAD_DIM)).astype(f32).astype(bf16)
    at_t = lax.broadcasted_iota(jnp.int32, (BLOCK, BLOCK), 0)
    at_s = lax.broadcasted_iota(jnp.int32, (BLOCK, BLOCK), 1)
    outs = (gated_f, gated_r)

    def keep(way):
        return at_t >= at_s if way == 0 else at_t <= at_s

    def rows_of(b):
        return pl.ds(pl.multiple_of(b * BLOCK, BLOCK), BLOCK)

    @pl.loop(0, blocks)
    def _(b):
        at = rows_of(b)
        val = values[at, :].astype(f32)
        b_rows = bc[at, 0:STATE]
        for way in range(2):
            x = step[at, :] + params[way : way + 1, :]
            dt = jnp.maximum(x, 0.0) + jnp.log1p(jnp.exp(-jnp.abs(x)))
            logd = -params[2 + way : 3 + way, :] * dt
            cum = jnp.dot(
                keep(way).astype(f32), logd,
                precision=lax.Precision.HIGHEST, preferred_element_type=f32,
            )
            total = cum[BLOCK - 1 : BLOCK, :] if way == 0 else cum[0:1, :]
            cums[way, b] = cum
            cums_t[way, b] = cum.T
            dts_t[way, b] = dt.T
            ends_log[way, b] = jnp.broadcast_to(total, (8, LANES))
            scaled = (val * expand(jnp.exp(total - cum) * dt, spread)).astype(bf16)
            states[way, b] = lax.dot_general(
                b_rows, scaled, (((0,), (0,)), ((), ())), preferred_element_type=f32
            )

    for way in range(2):
        end = states[way, 0 if way == 0 else blocks - 1]
        log = ends_log[way, 0 if way == 0 else blocks - 1]
        for i in range(1, blocks):
            b = i if way == 0 else blocks - 1 - i
            end = end * expand(jnp.exp(ends_log[way, b]), spread)[0:1] + states[way, b]
            log = log + ends_log[way, b]
        mine[way] = end.astype(bf16)
        my_logs[way] = log

    def send_state(target, slot):
        way = jnp.where(target > place, 0, 1)
        return pltpu.make_async_remote_copy(
            src_ref=mine.at[way], dst_ref=held.at[place], send_sem=send_sem.at[slot],
            recv_sem=recv_sem.at[place], device_id={"seq": target}, device_id_type=MESH,
        )

    def send_log(target, slot):
        way = jnp.where(target > place, 0, 1)
        return pltpu.make_async_remote_copy(
            src_ref=my_logs.at[way], dst_ref=logs.at[place], send_sem=log_send.at[slot],
            recv_sem=log_recv.at[place], device_id={"seq": target}, device_id_type=MESH,
        )

    def arrive(owner):
        pltpu.make_async_remote_copy(
            src_ref=mine.at[0], dst_ref=held.at[owner], send_sem=send_sem.at[0],
            recv_sem=recv_sem.at[owner], device_id={"seq": owner}, device_id_type=MESH,
        ).wait_recv()
        pltpu.make_async_remote_copy(
            src_ref=my_logs.at[0], dst_ref=logs.at[owner], send_sem=log_send.at[0],
            recv_sem=log_recv.at[owner], device_id={"seq": owner}, device_id_type=MESH,
        ).wait_recv()

    line_barrier("seq", count)
    for other in range(1, count):
        send_log(lax.rem(place + other, count), other).start()
        send_state(lax.rem(place + other, count), other).start()

    half = lax.broadcasted_iota(jnp.int32, (BLOCK, 2 * HEAD_DIM), 1) < HEAD_DIM

    @pl.loop(0, blocks)
    def _(b):
        at = rows_of(b)
        scores = lax.dot_general(
            bc[at, STATE : 2 * STATE], bc[at, 0:STATE], (((1,), (1,)), ((), ())),
            preferred_element_type=f32,
        )
        for way in range(2):
            masked_scores = jnp.where(keep(way), scores, 0.0)
            for pair in range(heads // 2):
                cols = slice(pair * 2 * HEAD_DIM, (pair + 1) * 2 * HEAD_DIM)
                val = values[at, cols]
                inside = []
                for h in (2 * pair, 2 * pair + 1):
                    differ = cums[way, b, :, h : h + 1] - cums_t[way, b, h : h + 1, :]
                    weight = jnp.exp(jnp.minimum(differ, 0.0)) * dts_t[way, b, h : h + 1, :]
                    inside.append(dot((masked_scores * weight).astype(bf16), val))
                outs[way][at, cols] = jnp.where(half, inside[0], inside[1])

    @pl.loop(0, count)
    def _(q):
        @pl.when(q != place)
        def _():
            arrive(q)

    enter[...] = jnp.zeros_like(enter)

    def step_in(way, q):
        factor = expand(jnp.exp(logs[q]), spread)[0:1]
        enter[way] = enter[way] * factor + held[q].astype(f32)

    @pl.loop(0, count)
    def _(i):
        @pl.when(i < place)
        def _():
            step_in(0, i)

        @pl.when(count - 1 - i > place)
        def _():
            step_in(1, count - 1 - i)

    @pl.loop(0, blocks)
    def _(i):
        for way in range(2):
            b = i if way == 0 else blocks - 1 - i
            at = rows_of(b)
            carried = dot(bc[at, STATE : 2 * STATE], enter[way].astype(bf16))
            skip = expand(jnp.broadcast_to(params[4 + way : 5 + way, :], (8, LANES)), spread)[0:1]
            out = (
                outs[way][at, :] + carried * expand(jnp.exp(cums[way, b]), spread)
                + skip * values[at, :].astype(f32)
            )
            outs[way][at, :] = out * gate[at, :].astype(f32)
            factor = expand(jnp.exp(ends_log[way, b]), spread)[0:1]
            enter[way] = enter[way] * factor + states[way, b]

    for other in range(1, count):
        send_state(lax.rem(place + other, count), other).wait_send()
        send_log(lax.rem(place + other, count), other).wait_send()


def scan(count, heads, values, gate, step, bc, params):
    rows, units = values.shape
    blocks = rows // BLOCK
    vmem = pl.BlockSpec(memory_space=pltpu.VMEM)
    out = jax.ShapeDtypeStruct((rows, units), f32)
    sems = pltpu.SemaphoreType.DMA((count,))
    return pl.pallas_call(
        functools.partial(scan_kernel, count, heads),
        out_shape=(out, out),
        in_specs=[vmem] * 5,
        out_specs=(vmem, vmem),
        scratch_shapes=[
            pltpu.VMEM((2, blocks, BLOCK, LANES), f32),
            pltpu.VMEM((2, blocks, LANES, BLOCK), f32),
            pltpu.VMEM((2, blocks, LANES, BLOCK), f32),
            pltpu.VMEM((2, blocks, 8, LANES), f32),
            pltpu.VMEM((2, blocks, STATE, units), f32),
            pltpu.VMEM((2, STATE, units), bf16),
            pltpu.VMEM((2, 8, LANES), f32),
            pltpu.VMEM((count, STATE, units), bf16),
            pltpu.VMEM((count, 8, LANES), f32),
            pltpu.VMEM((2, STATE, units), f32),
            sems, sems, sems, sems,
        ],
        compiler_params=pltpu.CompilerParams(
            collective_id=2, has_side_effects=True, vmem_limit_bytes=56 * 2**20
        ),
    )(values, gate, step, bc, params)


def on_device(
    hidden, masked, mask_embed, in_gain, w_gate, w_value, w_step, w_bc,
    dt_bias_forward, dt_bias_reverse, rate_forward, rate_reverse,
    skip_forward, skip_reverse, out_gain, w_out,
):
    n = lax.axis_size("head")
    heads = w_step.shape[1]
    more = LANES - heads
    gate_act, values, step_proj, bc = project(
        n, hidden, masked, mask_embed, in_gain, w_gate, w_value,
        jnp.pad(w_step, ((0, 0), (0, more))), w_bc,
    )
    params = jnp.stack(
        [dt_bias_forward, dt_bias_reverse, rate_forward, rate_reverse, skip_forward, skip_reverse]
    )
    params = jnp.pad(params, ((0, 2), (0, more)))
    gated_f, gated_r = scan(
        lax.axis_size("seq"), heads, values, gate_act, step_proj, bc, params
    )
    return project_out(n, HEADS * HEAD_DIM, gated_f, gated_r, out_gain, w_out)


def solution(mesh):
    head = P("head")
    in_specs = (
        P(("seq", "head"), None), P(("seq", "head")), P(), P(),
        P(None, "head"), P(None, "head"), P(None, "head"), P(),
        head, head, head, head, head, head, head, P("head", None),
    )
    return jax.shard_map(
        on_device, mesh=mesh, in_specs=in_specs,
        out_specs=P(("seq", "head"), None), check_vma=False,
    )
```

```python
import functools

import jax
import jax.numpy as jnp
from jax import lax
from jax.experimental import pallas as pl
from jax.experimental.pallas import tpu as pltpu
from jax.sharding import PartitionSpec as P

HEADS = 64
HEAD_DIM = 64
STATE = 128
BLOCK = 256
LANES = 128

epsilon = 1e-05
bf16 = jnp.bfloat16
f32 = jnp.float32
MESH = pl.DeviceIdType.MESH


def dot(a, b):
    return jnp.dot(a, b, preferred_element_type=f32)


def line_barrier(axis, n):
    me = lax.axis_index(axis)
    barrier = pltpu.get_barrier_semaphore()
    for other in range(1, n):
        pl.semaphore_signal(
            barrier, inc=1, device_id={axis: lax.rem(me + other, n)}, device_id_type=MESH
        )
    pl.semaphore_wait(barrier, n - 1)


def project_kernel(
    n, subs, hidden, masked, embed, in_gain, gate_hbm, value_hbm, step_hbm, bc_hbm,
    gate_out, value_out, step_out, bc_out,
    rows, w_gate, w_value, w_step, w_bc, load_sem, right_sem, left_sem, recv_sem,
):
    me = lax.axis_index("head")
    loads = [
        pltpu.make_async_copy(src, dst, load_sem.at[i])
        for i, (src, dst) in enumerate(
            ((bc_hbm, w_bc), (step_hbm, w_step), (value_hbm, w_value), (gate_hbm, w_gate))
        )
    ]
    for load in loads:
        load.start()
    count = hidden.shape[0]
    part = count // subs

    def copy(chunk, sub, send_sem, target):
        piece = rows.at[chunk, pl.ds(sub * part, part)]
        return pltpu.make_async_remote_copy(
            src_ref=piece, dst_ref=piece, send_sem=send_sem.at[chunk, sub],
            recv_sem=recv_sem.at[chunk, sub],
            device_id={"head": target}, device_id_type=MESH,
        )

    line_barrier("head", n)
    for sub in range(subs):
        own = pl.ds(sub * part, part)
        source = jnp.where(masked[own, :] == 1, embed[...], hidden[own, :]).astype(f32)
        mean = jnp.mean(source * source, axis=1, keepdims=True)
        rows[me, own, :] = (source * lax.rsqrt(mean + epsilon) * in_gain[...]).astype(bf16)

        @pl.when(me < n - 1)
        def _():
            copy(me, sub, right_sem, me + 1).start()

        @pl.when(me > 0)
        def _():
            copy(me, sub, left_sem, me - 1).start()

    for load in loads:
        load.wait()

    def compute(chunk):
        x = rows[chunk]
        at = pl.ds(pl.multiple_of(chunk * count, count), count)
        bc_out[at, :] = dot(x, w_bc[...]).astype(bf16)
        step_out[at, :] = dot(x, w_step[...])
        width = w_gate.shape[1]
        tile = 256 if width % 256 == 0 else width

        @pl.loop(0, width // tile)
        def _(i):
            cols = pl.ds(pl.multiple_of(i * tile, tile), tile)
            v = dot(x, w_value[:, cols])
            value_out[at, cols] = (v * jax.nn.sigmoid(v)).astype(bf16)
            g = dot(x, w_gate[:, cols])
            gate_out[at, cols] = (g * jax.nn.sigmoid(g)).astype(bf16)

    compute(me)

    @pl.loop(1, n)
    def _(d):
        for sub in range(subs):

            @pl.when(me - d >= 0)
            def _():
                copy(me - d, sub, right_sem, me).wait_recv()

                @pl.when(me < n - 1)
                def _():
                    copy(me - d, sub, right_sem, me + 1).start()

            @pl.when(me + d < n)
            def _():
                copy(me + d, sub, left_sem, me).wait_recv()

                @pl.when(me > 0)
                def _():
                    copy(me + d, sub, left_sem, me - 1).start()

        @pl.when(me - d >= 0)
        def _():
            compute(me - d)

        @pl.when(me + d < n)
        def _():
            compute(me + d)

    @pl.loop(0, n)
    def _(c):
        @pl.when((c <= me) & (me < n - 1))
        def _():
            for sub in range(subs):
                copy(c, sub, right_sem, me + 1).wait_send()

        @pl.when((c >= me) & (me > 0))
        def _():
            for sub in range(subs):
                copy(c, sub, left_sem, me - 1).wait_send()


def project(n, hidden, masked, mask_embed, in_gain, w_gate, w_value, w_step, w_bc):
    count, width = hidden.shape
    units, heads, both = w_gate.shape[1], w_step.shape[1], w_bc.shape[1]
    subs = 4
    total = n * count
    vmem, any_ = pl.BlockSpec(memory_space=pltpu.VMEM), pl.BlockSpec(memory_space=pl.ANY)
    sems = pltpu.SemaphoreType.DMA((n, subs))
    return pl.pallas_call(
        functools.partial(project_kernel, n, subs),
        out_shape=(
            jax.ShapeDtypeStruct((total, units), bf16),
            jax.ShapeDtypeStruct((total, units), bf16),
            jax.ShapeDtypeStruct((total, heads), f32),
            jax.ShapeDtypeStruct((total, both), bf16),
        ),
        in_specs=[vmem] * 4 + [any_] * 4,
        out_specs=(vmem,) * 4,
        scratch_shapes=[
            pltpu.VMEM((n, count, width), bf16),
            pltpu.VMEM(w_gate.shape, bf16), pltpu.VMEM(w_value.shape, bf16),
            pltpu.VMEM(w_step.shape, bf16), pltpu.VMEM(w_bc.shape, bf16),
            pltpu.SemaphoreType.DMA((4,)), sems, sems, sems,
        ],
        compiler_params=pltpu.CompilerParams(
            collective_id=0, has_side_effects=True, vmem_limit_bytes=56 * 2**20
        ),
    )(hidden, masked[:, None], mask_embed[None], in_gain[None], w_gate, w_value, w_step, w_bc)


def output_kernel(
    n, subs, inner, gated_f, gated_r, gain, w_hbm, out,
    w_out, both, sums, held, sent, load_sem, sum_send, sum_recv, send_sem, recv_sem,
):
    me = lax.axis_index("head")
    load = pltpu.make_async_copy(w_hbm, w_out, load_sem)
    load.start()
    count = out.shape[0]
    part = out.shape[1] // subs

    def row_sums(ref):
        g = ref[...]
        total = jnp.sum(g * g, axis=1, keepdims=True)
        return jnp.broadcast_to(total, (total.shape[0], LANES)).T[0:8]

    sums[me, 0:8, :] = row_sums(gated_f)
    sums[me, 8:16, :] = row_sums(gated_r)
    line_barrier("head", n)

    def share(owner, target, slot):
        return pltpu.make_async_remote_copy(
            src_ref=sums.at[owner], dst_ref=sums.at[owner], send_sem=sum_send.at[slot],
            recv_sem=sum_recv.at[owner], device_id={"head": target}, device_id_type=MESH,
        )

    for other in range(1, n):
        share(me, lax.rem(me + other, n), other).start()
    for other in range(1, n):
        owner = lax.rem(me + other, n)
        share(owner, owner, other).wait_recv()
    total = jnp.sum(sums[...], axis=0)
    scale = lax.rsqrt(total / inner + epsilon).T
    mixed = gated_f[...] * scale[:, 0:1] + gated_r[...] * scale[:, 8:9]
    both[...] = (mixed * gain[...]).astype(bf16)
    load.wait()

    def partial(dest, sub):
        at = pl.ds(pl.multiple_of(dest * count, count), count)
        return dot(both[at, :], w_out[:, pl.ds(pl.multiple_of(sub * part, part), part)])

    def send(dest, sub, way, target):
        return pltpu.make_async_remote_copy(
            src_ref=sent.at[dest, sub], dst_ref=held.at[way, dest, sub],
            send_sem=send_sem.at[dest, sub], recv_sem=recv_sem.at[way, dest, sub],
            device_id={"head": target}, device_id_type=MESH,
        )

    def pass_on(dest, sub, way, first, target):
        sent[dest, sub] = partial(dest, sub).astype(bf16)

        @pl.when(jnp.logical_not(first))
        def _():
            send(dest, sub, way, me).wait_recv()
            sent[dest, sub] = (
                sent[dest, sub].astype(f32) + held[way, dest, sub].astype(f32)
            ).astype(bf16)

        send(dest, sub, way, target).start()

    @pl.loop(0, (n - 1) * subs)
    def _(i):
        t, sub = i // subs, lax.rem(i, subs)

        @pl.when((t >= me) & (me < n - 1))
        def _():
            pass_on(n - 1 - t + me, sub, 0, me == 0, me + 1)

        @pl.when((t >= n - 1 - me) & (me > 0))
        def _():
            pass_on(t - (n - 1 - me), sub, 1, me == n - 1, me - 1)

    @pl.loop(0, subs)
    def _(sub):
        cols = pl.ds(pl.multiple_of(sub * part, part), part)
        out[:, cols] = partial(me, sub).astype(bf16)

        @pl.when(me > 0)
        def _():
            send(me, sub, 0, me).wait_recv()
            out[:, cols] = (out[:, cols].astype(f32) + held[0, me, sub].astype(f32)).astype(bf16)

        @pl.when(me < n - 1)
        def _():
            send(me, sub, 1, me).wait_recv()
            out[:, cols] = (out[:, cols].astype(f32) + held[1, me, sub].astype(f32)).astype(bf16)

    @pl.loop(0, n * subs)
    def _(i):
        dest, sub = i // subs, lax.rem(i, subs)

        @pl.when(dest != me)
        def _():
            send(dest, sub, 0, me).wait_send()

    for other in range(1, n):
        share(me, me, other).wait_send()


def project_out(n, inner, gated_f, gated_r, out_gain, w_out):
    rows, units = gated_f.shape
    width = w_out.shape[1]
    count = rows // n
    subs = 4
    vmem, any_ = pl.BlockSpec(memory_space=pltpu.VMEM), pl.BlockSpec(memory_space=pl.ANY)
    return pl.pallas_call(
        functools.partial(output_kernel, n, subs, inner),
        out_shape=jax.ShapeDtypeStruct((count, width), bf16),
        in_specs=[vmem] * 3 + [any_],
        out_specs=vmem,
        scratch_shapes=[
            pltpu.VMEM(w_out.shape, bf16),
            pltpu.VMEM((rows, units), bf16),
            pltpu.VMEM((n, 16, rows), f32),
            pltpu.VMEM((2, n, subs, count, width // subs), bf16),
            pltpu.VMEM((n, subs, count, width // subs), bf16),
            pltpu.SemaphoreType.DMA, pltpu.SemaphoreType.DMA((n,)),
            pltpu.SemaphoreType.DMA((n,)), pltpu.SemaphoreType.DMA((n, subs)),
            pltpu.SemaphoreType.DMA((2, n, subs)),
        ],
        compiler_params=pltpu.CompilerParams(
            collective_id=1, has_side_effects=True, vmem_limit_bytes=56 * 2**20
        ),
    )(gated_f, gated_r, out_gain[None], w_out)


def expand(x, spread):
    high = x.astype(bf16)
    return dot(high, spread) + dot((x - high.astype(f32)).astype(bf16), spread)


def scan_kernel(
    count, heads, values, gate, step, bc, params, gated_f, gated_r,
    cums, cums_t, dts_t, ends_log, states, mine, my_logs, held, logs, enter,
    send_sem, recv_sem, log_send, log_recv,
):
    place = lax.axis_index("seq")
    rows, units = values.shape
    blocks = rows // BLOCK
    lane_of = lax.broadcasted_iota(jnp.int32, (LANES, units), 1)
    head_of = lax.broadcasted_iota(jnp.int32, (LANES, units), 0) * HEAD_DIM
    spread = ((lane_of >= head_of) & (lane_of < head_of + HEAD_DIM)).astype(f32).astype(bf16)
    at_t = lax.broadcasted_iota(jnp.int32, (BLOCK, BLOCK), 0)
    at_s = lax.broadcasted_iota(jnp.int32, (BLOCK, BLOCK), 1)
    outs = (gated_f, gated_r)

    def keep(way):
        return at_t >= at_s if way == 0 else at_t <= at_s

    def rows_of(b):
        return pl.ds(pl.multiple_of(b * BLOCK, BLOCK), BLOCK)

    @pl.loop(0, blocks)
    def _(b):
        at = rows_of(b)
        val = values[at, :].astype(f32)
        b_rows = bc[at, 0:STATE]
        for way in range(2):
            x = step[at, :] + params[way : way + 1, :]
            dt = jnp.maximum(x, 0.0) + jnp.log1p(jnp.exp(-jnp.abs(x)))
            logd = -params[2 + way : 3 + way, :] * dt
            cum = jnp.dot(
                keep(way).astype(f32), logd,
                precision=lax.Precision.HIGHEST, preferred_element_type=f32,
            )
            total = cum[BLOCK - 1 : BLOCK, :] if way == 0 else cum[0:1, :]
            cums[way, b] = cum
            cums_t[way, b] = cum.T
            dts_t[way, b] = dt.T
            ends_log[way, b] = jnp.broadcast_to(total, (8, LANES))
            scaled = (val * expand(jnp.exp(total - cum) * dt, spread)).astype(bf16)
            states[way, b] = lax.dot_general(
                b_rows, scaled, (((0,), (0,)), ((), ())), preferred_element_type=f32
            )

    for way in range(2):
        end = states[way, 0 if way == 0 else blocks - 1]
        log = ends_log[way, 0 if way == 0 else blocks - 1]
        for i in range(1, blocks):
            b = i if way == 0 else blocks - 1 - i
            end = end * expand(jnp.exp(ends_log[way, b]), spread)[0:1] + states[way, b]
            log = log + ends_log[way, b]
        mine[way] = end.astype(bf16)
        my_logs[way] = log

    def send_state(target, slot):
        way = jnp.where(target > place, 0, 1)
        return pltpu.make_async_remote_copy(
            src_ref=mine.at[way], dst_ref=held.at[place], send_sem=send_sem.at[slot],
            recv_sem=recv_sem.at[place], device_id={"seq": target}, device_id_type=MESH,
        )

    def send_log(target, slot):
        way = jnp.where(target > place, 0, 1)
        return pltpu.make_async_remote_copy(
            src_ref=my_logs.at[way], dst_ref=logs.at[place], send_sem=log_send.at[slot],
            recv_sem=log_recv.at[place], device_id={"seq": target}, device_id_type=MESH,
        )

    def arrive(owner):
        pltpu.make_async_remote_copy(
            src_ref=mine.at[0], dst_ref=held.at[owner], send_sem=send_sem.at[0],
            recv_sem=recv_sem.at[owner], device_id={"seq": owner}, device_id_type=MESH,
        ).wait_recv()
        pltpu.make_async_remote_copy(
            src_ref=my_logs.at[0], dst_ref=logs.at[owner], send_sem=log_send.at[0],
            recv_sem=log_recv.at[owner], device_id={"seq": owner}, device_id_type=MESH,
        ).wait_recv()

    line_barrier("seq", count)
    for other in range(1, count):
        send_log(lax.rem(place + other, count), other).start()
        send_state(lax.rem(place + other, count), other).start()

    half = lax.broadcasted_iota(jnp.int32, (BLOCK, 2 * HEAD_DIM), 1) < HEAD_DIM

    @pl.loop(0, blocks)
    def _(b):
        at = rows_of(b)
        scores = lax.dot_general(
            bc[at, STATE : 2 * STATE], bc[at, 0:STATE], (((1,), (1,)), ((), ())),
            preferred_element_type=f32,
        )
        for way in range(2):
            masked_scores = jnp.where(keep(way), scores, 0.0)
            for pair in range(heads // 2):
                cols = slice(pair * 2 * HEAD_DIM, (pair + 1) * 2 * HEAD_DIM)
                val = values[at, cols]
                inside = []
                for h in (2 * pair, 2 * pair + 1):
                    differ = cums[way, b, :, h : h + 1] - cums_t[way, b, h : h + 1, :]
                    weight = jnp.exp(jnp.minimum(differ, 0.0)) * dts_t[way, b, h : h + 1, :]
                    inside.append(dot((masked_scores * weight).astype(bf16), val))
                outs[way][at, cols] = jnp.where(half, inside[0], inside[1])

    @pl.loop(0, count)
    def _(q):
        @pl.when(q != place)
        def _():
            arrive(q)

    enter[...] = jnp.zeros_like(enter)

    def step_in(way, q):
        factor = expand(jnp.exp(logs[q]), spread)[0:1]
        enter[way] = enter[way] * factor + held[q].astype(f32)

    @pl.loop(0, count)
    def _(i):
        @pl.when(i < place)
        def _():
            step_in(0, i)

        @pl.when(count - 1 - i > place)
        def _():
            step_in(1, count - 1 - i)

    @pl.loop(0, blocks)
    def _(i):
        for way in range(2):
            b = i if way == 0 else blocks - 1 - i
            at = rows_of(b)
            carried = dot(bc[at, STATE : 2 * STATE], enter[way].astype(bf16))
            skip = expand(jnp.broadcast_to(params[4 + way : 5 + way, :], (8, LANES)), spread)[0:1]
            out = (
                outs[way][at, :] + carried * expand(jnp.exp(cums[way, b]), spread)
                + skip * values[at, :].astype(f32)
            )
            outs[way][at, :] = out * gate[at, :].astype(f32)
            factor = expand(jnp.exp(ends_log[way, b]), spread)[0:1]
            enter[way] = enter[way] * factor + states[way, b]

    for other in range(1, count):
        send_state(lax.rem(place + other, count), other).wait_send()
        send_log(lax.rem(place + other, count), other).wait_send()


def scan(count, heads, values, gate, step, bc, params):
    rows, units = values.shape
    blocks = rows // BLOCK
    vmem = pl.BlockSpec(memory_space=pltpu.VMEM)
    out = jax.ShapeDtypeStruct((rows, units), f32)
    sems = pltpu.SemaphoreType.DMA((count,))
    return pl.pallas_call(
        functools.partial(scan_kernel, count, heads),
        out_shape=(out, out),
        in_specs=[vmem] * 5,
        out_specs=(vmem, vmem),
        scratch_shapes=[
            pltpu.VMEM((2, blocks, BLOCK, LANES), f32),
            pltpu.VMEM((2, blocks, LANES, BLOCK), f32),
            pltpu.VMEM((2, blocks, LANES, BLOCK), f32),
            pltpu.VMEM((2, blocks, 8, LANES), f32),
            pltpu.VMEM((2, blocks, STATE, units), f32),
            pltpu.VMEM((2, STATE, units), bf16),
            pltpu.VMEM((2, 8, LANES), f32),
            pltpu.VMEM((count, STATE, units), bf16),
            pltpu.VMEM((count, 8, LANES), f32),
            pltpu.VMEM((2, STATE, units), f32),
            sems, sems, sems, sems,
        ],
        compiler_params=pltpu.CompilerParams(
            collective_id=2, has_side_effects=True, vmem_limit_bytes=56 * 2**20
        ),
    )(values, gate, step, bc, params)


def on_device(
    hidden, masked, mask_embed, in_gain, w_gate, w_value, w_step, w_bc,
    dt_bias_forward, dt_bias_reverse, rate_forward, rate_reverse,
    skip_forward, skip_reverse, out_gain, w_out,
):
    n = lax.axis_size("head")
    heads = w_step.shape[1]
    more = LANES - heads
    gate_act, values, step_proj, bc = project(
        n, hidden, masked, mask_embed, in_gain, w_gate, w_value,
        jnp.pad(w_step, ((0, 0), (0, more))), w_bc,
    )
    params = jnp.stack(
        [dt_bias_forward, dt_bias_reverse, rate_forward, rate_reverse, skip_forward, skip_reverse]
    )
    params = jnp.pad(params, ((0, 2), (0, more)))
    gated_f, gated_r = scan(
        lax.axis_size("seq"), heads, values, gate_act, step_proj, bc, params
    )
    return project_out(n, HEADS * HEAD_DIM, gated_f, gated_r, out_gain, w_out)


def solution(mesh):
    head = P("head")
    in_specs = (
        P(("seq", "head"), None), P(("seq", "head")), P(), P(),
        P(None, "head"), P(None, "head"), P(None, "head"), P(),
        head, head, head, head, head, head, head, P("head", None),
    )
    return jax.shard_map(
        on_device, mesh=mesh, in_specs=in_specs,
        out_specs=P(("seq", "head"), None), check_vma=False,
    )
```
